32 devices in a mesh: sector: 8 (over y, x, core), op: 4 (over z).
Axes of the slice: x: 2, y: 2, z: 4, core: 2. Of those that a mesh axis runs over, the one named last changes fastest.
Arguments:
- wave: bfloat16 [512, 768], P('sector'), may hold values from -6 to 6
- left_blocks: bfloat16 [24, 512, 64], P('op', 'sector'), may hold values from -0.75 to 0.75
- right_ops: bfloat16 [24, 768, 768], P('op'), may hold values from -0.21875 to 0.21875
- delta: int32 [24], P('op'), may hold values from -1 to 1
- active: int32 [24, 8], P('op', 'sector'), may hold values 0 or 1
- sector_rows: int32 [8], P('sector'), may hold values from 16 to 64
Outputs:
- sigma: bfloat16 [512, 768], P('sector', 'op')
The draws below stay inside these ranges and needn't reach their ends.
All inputs are finite; a program needn't handle non-finite values. No bound on the sum of `active` on one device may be relied on, other than what follows from the above.
Results may differ from the reference program's by a relative error of at most 0.011.
Values sent between devices are 32-bit elements; how exact they have to be, the bound alone decides.
A program may use at most 64 MiB of HBM per device.

```python
import jax
import jax.numpy as jnp
from jax import lax

RS = 768
ROW_DEV = 64
SECTORS = 8
OPS = 24


def draw_sector_rows(key, part):
    key = jax.random.fold_in(key, 7)
    first, second = jax.random.split(key)
    sizes = jax.random.randint(first, (SECTORS,), ROW_DEV // 4, ROW_DEV + 1)
    place = jax.random.randint(second, (), 0, SECTORS)
    sizes = jnp.where(jnp.arange(SECTORS) == place, ROW_DEV, sizes)
    return sizes.astype(jnp.int32)


def touch_ends(result, key, least, top_value):
    spot = [jax.random.randint(jax.random.fold_in(key, axis), (), 0, length) for axis, length in enumerate(result.shape)]
    longest = result.shape.index(max(result.shape))
    next_to = spot[:longest] + [(spot[longest] + 1) % result.shape[longest]] + spot[longest + 1:]
    return result.at[tuple(spot)].set(least).at[tuple(next_to)].set(top_value)


def steps_of(own_key, extent, pieces, low, high):
    level = 1.0
    for dim, shards_of in pieces:
        draws = jax.random.uniform(jax.random.fold_in(jax.random.fold_in(own_key, 6), dim), (shards_of,), jnp.float32, low / len(pieces), high / len(pieces))
        level = level * jnp.repeat(jnp.exp(draws), extent[dim] // shards_of).reshape((-1,) + (1,) * (len(extent) - 1 - dim))
    return level


def centred(key, extent, width, bound, pieces=(), held_as=jnp.bfloat16):
    array = jax.random.normal(key, extent, jnp.float32) * width
    if len(pieces) > 0:
        array = steps_of(key, extent, pieces, -0.22, 0.18) * array
    return jnp.clip(array, min=-bound, max=bound).astype(held_as)


def setup_inputs(seed: int = 0) -> dict:
    key_list = jax.random.split(jax.random.key(seed), 7)
    wave = centred(key_list[0], (SECTORS * ROW_DEV, RS), 1.0, 6.0, ((0, 8),))
    left_blocks = centred(key_list[1], (OPS, SECTORS * ROW_DEV, ROW_DEV), ROW_DEV ** -0.5, 0.75, ((0, 4), (1, 8)))
    right_ops = centred(key_list[2], (OPS, RS, RS), RS ** -0.5, 0.21875, ((0, 4),))
    delta = touch_ends(jax.random.randint(key_list[3], (OPS,), -1, 2), jax.random.fold_in(key_list[3], 1), -1, 1).astype(jnp.int32)
    active = touch_ends((jax.random.randint(key_list[4], (OPS, SECTORS), 0, 2) < 1).astype(jnp.int32), jax.random.fold_in(key_list[4], 1), 0, 1)
    sector_rows = draw_sector_rows(jax.random.fold_in(key_list[6], 71), 0)
    return {"wave": wave, "left_blocks": left_blocks, "right_ops": right_ops, "delta": delta, "active": active, "sector_rows": sector_rows}


def reference(wave, left_blocks, right_ops, delta, active, sector_rows):
    rows = jnp.arange(ROW_DEV, dtype=jnp.int32)
    live = rows[None, :] < sector_rows[:, None]
    blocks = wave.reshape(SECTORS, ROW_DEV, RS)
    masked = jnp.where(live[:, :, None], blocks, jnp.zeros_like(blocks))
    masked_f = masked.astype(jnp.float32)
    lefts = left_blocks.reshape(OPS, SECTORS, ROW_DEV, ROW_DEV)

    def one_op(acc, items):
        left_k, right_k, delta_k, active_k = items
        inter = jnp.einsum('sij,sjc->sic', left_k.astype(jnp.float32), masked_f)
        inter = inter.astype(jnp.bfloat16).astype(jnp.float32)
        term = jnp.einsum('sic,cd->sid', inter, right_k.astype(jnp.float32))
        term = term * active_k.astype(jnp.float32)[:, None, None]
        picks = (jnp.arange(3, dtype=jnp.int32) == delta_k + 1).astype(jnp.float32)
        return acc + picks[:, None, None, None] * term[None], None

    acc = jnp.zeros((3, SECTORS, ROW_DEV, RS), jnp.float32)
    acc, _ = lax.scan(one_op, acc, (lefts, right_ops, delta, active))
    zero_block = jnp.zeros((1, ROW_DEV, RS), jnp.float32)
    from_below = jnp.concatenate([zero_block, acc[2][:-1]], axis=0)
    from_above = jnp.concatenate([acc[0][1:], zero_block], axis=0)
    total = acc[1] + from_below + from_above
    total = jnp.where(live[:, :, None], total, 0.0)
    return total.reshape(SECTORS * ROW_DEV, RS).astype(jnp.bfloat16)
```

```python
import functools

import jax
import jax.numpy as jnp
from jax import lax
from jax.experimental import pallas as pl
from jax.experimental.pallas import tpu as pltpu
from jax.sharding import PartitionSpec as P

MESH = pl.DeviceIdType.MESH
LANES = 128


def layout(columns, n_op):
    width = columns // n_op
    plan, most = [], 0
    for q in range(n_op):
        pieces = []
        for tile in range(columns // LANES):
            lo, hi = max(q * width, tile * LANES), min((q + 1) * width, (tile + 1) * LANES)
            if lo < hi:
                pieces.append((tile, lo - tile * LANES, hi - tile * LANES))
        placed, at = {}, 0
        for piece in sorted(pieces, key=lambda p: p[1] - p[2]):
            rows = 32 if piece[2] - piece[1] == 64 else 64
            placed[piece] = (at, rows)
            at += rows
        plan.append([p + placed[p] for p in pieces])
        most = max(most, at)
    return plan, most


def pack(block, lo, hi):
    part = block[:, lo:hi]
    if hi - lo == LANES:
        return part
    if hi - lo == 64:
        return jnp.concatenate([part[:32], part[32:]], axis=1)
    return jnp.concatenate([part, jnp.zeros((part.shape[0], LANES - hi + lo), part.dtype)], axis=1)


def unpack(rows, width):
    if width == LANES:
        return rows
    if width == 64:
        return jnp.concatenate([rows[:, :64], rows[:, 64:]], axis=0)
    return rows[:, :width]


def kernel(n_sector, n_op, wave, left, right, delta, active, live, out,
           lhs, held, keep, up, down, below, above, zsend, zrecv,
           load_sem, up_send, up_recv, down_send, down_recv, z_send, z_recv):
    s, me = lax.axis_index("sector"), lax.axis_index("op")
    ops, rows, _ = left.shape
    columns = wave.shape[1]
    tiles = columns // LANES
    chunks = tiles // 2
    plan, most = layout(columns, n_op)

    loads = []
    for c in range(chunks):
        pair = []
        for half, tile in enumerate((c, tiles - 1 - c)):
            load = pltpu.make_async_copy(
                right.at[:, tile * LANES:(tile + 1) * LANES],
                held.at[c, :, half * LANES:(half + 1) * LANES],
                load_sem.at[c, half])
            load.start()
            pair.append(load)
        loads.append(pair)

    barrier = pltpu.get_barrier_semaphore()

    @pl.when(s > 0)
    def _():
        pl.semaphore_signal(barrier, inc=1, device_id={"sector": s - 1}, device_id_type=MESH)

    @pl.when(s < n_sector - 1)
    def _():
        pl.semaphore_signal(barrier, inc=1, device_id={"sector": s + 1}, device_id_type=MESH)

    for hop in range(1, n_op):
        pl.semaphore_signal(barrier, inc=1, device_id={"op": lax.rem(me + hop, n_op)}, device_id_type=MESH)

    on_rows = lax.broadcasted_iota(jnp.int32, (rows, columns), 0) < live[0]
    masked = jnp.where(on_rows, wave[...].astype(jnp.float32), 0.0).astype(jnp.bfloat16)
    for k in range(ops):
        inter = jnp.dot(left[k], masked, preferred_element_type=jnp.float32)
        weight = active[k].astype(jnp.float32)
        for slot, change in enumerate((0, 1, -1)):
            picked = jnp.where(delta[k] == change, weight, 0.0)
            lhs[slot * rows:(slot + 1) * rows, k * columns:(k + 1) * columns] = (inter * picked).astype(jnp.bfloat16)

    @pl.when(s == 0)
    def _():
        below[...] = jnp.zeros_like(below)

    @pl.when(s == n_sector - 1)
    def _():
        above[...] = jnp.zeros_like(above)

    near = jnp.minimum(s, 1) + jnp.minimum(n_sector - 1 - s, 1)
    pl.semaphore_wait(barrier, n_op - 1 + near)

    def to_next(c):
        return pltpu.make_async_remote_copy(
            src_ref=up.at[c], dst_ref=below.at[c], send_sem=up_send.at[c], recv_sem=up_recv.at[c],
            device_id={"sector": s + 1}, device_id_type=MESH)

    def to_previous(c):
        return pltpu.make_async_remote_copy(
            src_ref=down.at[c], dst_ref=above.at[c], send_sem=down_send.at[c], recv_sem=down_recv.at[c],
            device_id={"sector": s - 1}, device_id_type=MESH)

    def to_shard(q, index):
        _, _, _, at, size = plan[q][index]
        slot = lax.rem(me - q + n_op, n_op) - 1
        return pltpu.make_async_remote_copy(
            src_ref=zsend.at[q, at:at + size], dst_ref=zrecv.at[slot, at:at + size],
            send_sem=z_send.at[q, index], recv_sem=z_recv.at[slot, index],
            device_id={"op": q}, device_id_type=MESH)

    def from_shard(q, index, slot):
        _, _, _, at, size = plan[q][index]
        return pltpu.make_async_remote_copy(
            src_ref=zsend.at[q, at:at + size], dst_ref=zrecv.at[slot, at:at + size],
            send_sem=z_send.at[q, index], recv_sem=z_recv.at[slot, index],
            device_id={"op": lax.rem(me + slot + 1, n_op)}, device_id_type=MESH)

    def compute(c):
        for load in loads[c]:
            load.wait()
        part = jnp.dot(lhs[...], held[c], preferred_element_type=jnp.float32)
        keep[c] = part[:rows]
        up[c] = part[rows:2 * rows]
        down[c] = part[2 * rows:]

        @pl.when(s < n_sector - 1)
        def _():
            to_next(c).start()

        @pl.when(s > 0)
        def _():
            to_previous(c).start()

    def combine(c):
        @pl.when(s > 0)
        def _():
            to_next(c).wait_recv()

        @pl.when(s < n_sector - 1)
        def _():
            to_previous(c).wait_recv()

        total = keep[c] + below[c] + above[c]
        for q in range(n_op):
            for index, (tile, lo, hi, at, size) in enumerate(plan[q]):
                if tile not in (c, tiles - 1 - c):
                    continue
                half = 0 if tile == c else 1
                zsend[q, at:at + size] = pack(total[:, half * LANES:(half + 1) * LANES], lo, hi)

                @pl.when(me != q)
                def _():
                    to_shard(q, index).start()

    for c in range(chunks):
        compute(c)
        if c > 0:
            combine(c - 1)
    combine(chunks - 1)

    for q in range(n_op):
        @pl.when(me == q)
        def _():
            for slot in range(n_op - 1):
                for index in range(len(plan[q])):
                    from_shard(q, index, slot).wait_recv()
            blocks = []
            for tile, lo, hi, at, size in plan[q]:
                whole = zsend[q, at:at + size]
                for slot in range(n_op - 1):
                    whole = whole + zrecv[slot, at:at + size]
                blocks.append(unpack(whole, hi - lo))
            block = blocks[0] if len(blocks) == 1 else jnp.concatenate(blocks, axis=1)
            shown = lax.broadcasted_iota(jnp.int32, block.shape, 0) < live[0]
            out[...] = jnp.where(shown, block, 0.0).astype(out.dtype)

        @pl.when(me != q)
        def _():
            for index in range(len(plan[q])):
                to_shard(q, index).wait_send()

    @pl.when(s < n_sector - 1)
    def _():
        for c in range(chunks):
            to_next(c).wait_send()

    @pl.when(s > 0)
    def _():
        for c in range(chunks):
            to_previous(c).wait_send()


def on_device(n_sector, n_op, wave, left_blocks, right_ops, delta, active, sector_rows):
    rows, columns = wave.shape
    ops = right_ops.shape[0]
    chunks = columns // (2 * LANES)
    plan, most = layout(columns, n_op)
    pieces = max(len(p) for p in plan)
    piece = pltpu.VMEM((chunks, rows, 2 * LANES), jnp.float32)
    vmem, smem = pl.BlockSpec(memory_space=pltpu.VMEM), pl.BlockSpec(memory_space=pltpu.SMEM)
    dma = pltpu.SemaphoreType.DMA
    return pl.pallas_call(
        functools.partial(kernel, n_sector, n_op),
        out_shape=jax.ShapeDtypeStruct((rows, columns // n_op), jnp.bfloat16),
        in_specs=[vmem, vmem, pl.BlockSpec(memory_space=pl.ANY), smem, smem, smem],
        out_specs=vmem,
        scratch_shapes=[
            pltpu.VMEM((3 * rows, ops * columns), jnp.bfloat16),
            pltpu.VMEM((chunks, ops * columns, 2 * LANES), jnp.bfloat16),
            piece, piece, piece, piece, piece,
            pltpu.VMEM((n_op, most, LANES), jnp.float32),
            pltpu.VMEM((n_op - 1, most, LANES), jnp.float32),
            dma((chunks, 2)),
            dma((chunks,)), dma((chunks,)), dma((chunks,)), dma((chunks,)),
            dma((n_op, pieces)), dma((n_op - 1, pieces)),
        ],
        compiler_params=pltpu.CompilerParams(
            collective_id=0, has_side_effects=True, vmem_limit_bytes=60 * 1024 * 1024),
        name="sigma_step",
    )(wave, left_blocks, right_ops.reshape(ops * columns, columns), delta, active.reshape(ops), sector_rows)


def solution(mesh):
    return jax.shard_map(
        functools.partial(on_device, mesh.shape["sector"], mesh.shape["op"]),
        mesh=mesh,
        in_specs=(
            P("sector", None),
            P("op", "sector", None),
            P("op", None, None),
            P("op"),
            P("op", "sector"),
            P("sector"),
        ),
        out_specs=P("sector", "op"),
        check_vma=False,
    )
```

```python
import functools

import jax
import jax.numpy as jnp
from jax import lax
from jax.experimental import pallas as pl
from jax.experimental.pallas import tpu as pltpu
from jax.sharding import PartitionSpec as P

MESH = pl.DeviceIdType.MESH
LANES = 128


def layout(columns, n_op):
    width = columns // n_op
    plan, most = [], 0
    for q in range(n_op):
        pieces = []
        for tile in range(columns // LANES):
            lo, hi = max(q * width, tile * LANES), min((q + 1) * width, (tile + 1) * LANES)
            if lo < hi:
                pieces.append((tile, lo - tile * LANES, hi - tile * LANES))
        placed, at = {}, 0
        for piece in sorted(pieces, key=lambda p: p[1] - p[2]):
            rows = 32 if piece[2] - piece[1] == 64 else 64
            placed[piece] = (at, rows)
            at += rows
        plan.append([p + placed[p] for p in pieces])
        most = max(most, at)
    return plan, most


def pack(block, lo, hi):
    part = block[:, lo:hi]
    if hi - lo == LANES:
        return part
    if hi - lo == 64:
        return jnp.concatenate([part[:32], part[32:]], axis=1)
    return jnp.concatenate([part, jnp.zeros((part.shape[0], LANES - hi + lo), part.dtype)], axis=1)


def unpack(rows, width):
    if width == LANES:
        return rows
    if width == 64:
        return jnp.concatenate([rows[:, :64], rows[:, 64:]], axis=0)
    return rows[:, :width]


def kernel(n_sector, n_op, wave_hbm, left_hbm, right, delta_hbm, active_hbm, live_hbm, out,
           wave, left, delta, active, live, inter, held, keep, up, down, below, above, zsend, zrecv,
           load_sem, small_sem, up_send, up_recv, down_send, down_recv, z_send, z_recv):
    s, me = lax.axis_index("sector"), lax.axis_index("op")
    ops, rows, _ = left.shape
    columns = wave.shape[1]
    tiles = columns // LANES
    chunks = tiles // 2
    plan, most = layout(columns, n_op)
    order = [tile for c in range(chunks) for tile in (c, tiles - 1 - c)]

    barrier = pltpu.get_barrier_semaphore()

    @pl.when(s > 0)
    def _():
        pl.semaphore_signal(barrier, inc=1, device_id={"sector": s - 1}, device_id_type=MESH)

    @pl.when(s < n_sector - 1)
    def _():
        pl.semaphore_signal(barrier, inc=1, device_id={"sector": s + 1}, device_id_type=MESH)

    for hop in range(1, n_op):
        pl.semaphore_signal(barrier, inc=1, device_id={"op": lax.rem(me + hop, n_op)}, device_id_type=MESH)

    small = []
    for i, (src, dst) in enumerate(((wave_hbm, wave), (left_hbm, left), (delta_hbm, delta),
                                    (active_hbm, active), (live_hbm, live))):
        small.append(pltpu.make_async_copy(src, dst, small_sem.at[i]))
        small[-1].start()

    loads = {}
    for c in range(chunks):
        for k in range(ops):
            pair = []
            for half in range(2):
                tile = order[2 * c + half]
                load = pltpu.make_async_copy(
                    right.at[k, :, tile * LANES:(tile + 1) * LANES],
                    held.at[c, k, :, half * LANES:(half + 1) * LANES],
                    load_sem.at[c, k, half])
                load.start()
                pair.append(load)
            loads[c, k] = pair

    @pl.when(s == 0)
    def _():
        below[...] = jnp.zeros_like(below)

    @pl.when(s == n_sector - 1)
    def _():
        above[...] = jnp.zeros_like(above)

    for load in small:
        load.wait()
    on_rows = lax.broadcasted_iota(jnp.int32, (rows, columns), 0) < live[0]
    masked = jnp.where(on_rows, wave[...].astype(jnp.float32), 0.0).astype(jnp.bfloat16)
    for k in range(ops):
        inter[k] = jnp.dot(left[k], masked, preferred_element_type=jnp.float32).astype(jnp.bfloat16)
    weights = [[jnp.where(delta[k] == change, active[k], 0).astype(jnp.float32) for k in range(ops)]
               for change in (0, 1, -1)]

    def to_next(i):
        return pltpu.make_async_remote_copy(
            src_ref=up.at[i], dst_ref=below.at[i], send_sem=up_send.at[i], recv_sem=up_recv.at[i],
            device_id={"sector": s + 1}, device_id_type=MESH)

    def to_previous(i):
        return pltpu.make_async_remote_copy(
            src_ref=down.at[i], dst_ref=above.at[i], send_sem=down_send.at[i], recv_sem=down_recv.at[i],
            device_id={"sector": s - 1}, device_id_type=MESH)

    def to_shard(q, index):
        _, _, _, at, size = plan[q][index]
        slot = lax.rem(me - q + n_op, n_op) - 1
        return pltpu.make_async_remote_copy(
            src_ref=zsend.at[q, at:at + size], dst_ref=zrecv.at[slot, at:at + size],
            send_sem=z_send.at[q, index], recv_sem=z_recv.at[slot, index],
            device_id={"op": q}, device_id_type=MESH)

    def from_shard(q, index, slot):
        _, _, _, at, size = plan[q][index]
        return pltpu.make_async_remote_copy(
            src_ref=zsend.at[q, at:at + size], dst_ref=zrecv.at[slot, at:at + size],
            send_sem=z_send.at[q, index], recv_sem=z_recv.at[slot, index],
            device_id={"op": lax.rem(me + slot + 1, n_op)}, device_id_type=MESH)

    def compute(c):
        sums = [None] * 3
        for k in range(ops):
            for load in loads[c, k]:
                load.wait()
            term = jnp.dot(inter[k], held[c, k], preferred_element_type=jnp.float32)
            for d in range(3):
                scaled = term * weights[d][k]
                sums[d] = scaled if k == 0 else sums[d] + scaled
        for half in range(2):
            at = slice(half * LANES, (half + 1) * LANES)
            i = 2 * c + half
            up[i] = sums[1][:, at]
            down[i] = sums[2][:, at]
            keep[i] = sums[0][:, at]

        if c == 0:
            near = jnp.minimum(s, 1) + jnp.minimum(n_sector - 1 - s, 1)
            pl.semaphore_wait(barrier, n_op - 1 + near)

        @pl.when(s < n_sector - 1)
        def _():
            for i in (2 * c, 2 * c + 1):
                to_next(i).start()

        @pl.when(s > 0)
        def _():
            for i in (2 * c, 2 * c + 1):
                to_previous(i).start()

    def combine(i):
        @pl.when(s > 0)
        def _():
            to_next(i).wait_recv()

        @pl.when(s < n_sector - 1)
        def _():
            to_previous(i).wait_recv()

        total = keep[i] + below[i] + above[i]
        for q in range(n_op):
            for index, (tile, lo, hi, at, size) in enumerate(plan[q]):
                if tile != order[i]:
                    continue
                zsend[q, at:at + size] = pack(total, lo, hi)

                @pl.when(me != q)
                def _():
                    to_shard(q, index).start()

    for c in range(chunks):
        compute(c)
    for i in range(tiles):
        combine(i)

    for q in range(n_op):
        @pl.when(me == q)
        def _():
            for slot in range(n_op - 1):
                for index in range(len(plan[q])):
                    from_shard(q, index, slot).wait_recv()
            blocks = []
            for tile, lo, hi, at, size in plan[q]:
                whole = zsend[q, at:at + size]
                for slot in range(n_op - 1):
                    whole = whole + zrecv[slot, at:at + size]
                blocks.append(unpack(whole, hi - lo))
            block = blocks[0] if len(blocks) == 1 else jnp.concatenate(blocks, axis=1)
            shown = lax.broadcasted_iota(jnp.int32, block.shape, 0) < live[0]
            out[...] = jnp.where(shown, block, 0.0)

        @pl.when(me != q)
        def _():
            for index in range(len(plan[q])):
                to_shard(q, index).wait_send()

    @pl.when(s < n_sector - 1)
    def _():
        for i in range(tiles):
            to_next(i).wait_send()

    @pl.when(s > 0)
    def _():
        for i in range(tiles):
            to_previous(i).wait_send()


def on_device(n_sector, n_op, wave, left_blocks, right_ops, delta, active, sector_rows):
    rows, columns = wave.shape
    ops = right_ops.shape[0]
    tiles = columns // LANES
    chunks = tiles // 2
    plan, most = layout(columns, n_op)
    pieces = max(len(p) for p in plan)
    piece = pltpu.VMEM((tiles, rows, LANES), jnp.float32)
    dma = pltpu.SemaphoreType.DMA
    block = pl.pallas_call(
        functools.partial(kernel, n_sector, n_op),
        out_shape=pltpu.VMEM((rows, columns // n_op), jnp.float32),
        in_specs=[pl.BlockSpec(memory_space=pltpu.HBM)] * 6,
        out_specs=pl.BlockSpec(memory_space=pltpu.VMEM),
        scratch_shapes=[
            pltpu.VMEM(wave.shape, wave.dtype),
            pltpu.VMEM(left_blocks.shape, left_blocks.dtype),
            pltpu.SMEM((ops,), jnp.int32),
            pltpu.SMEM((ops,), jnp.int32),
            pltpu.SMEM((1,), jnp.int32),
            pltpu.VMEM((ops, rows, columns), jnp.bfloat16),
            pltpu.VMEM((chunks, ops, columns, 2 * LANES), jnp.bfloat16),
            piece, piece, piece, piece, piece,
            pltpu.VMEM((n_op, most, LANES), jnp.float32),
            pltpu.VMEM((n_op - 1, most, LANES), jnp.float32),
            dma((chunks, ops, 2)), dma((5,)),
            dma((tiles,)), dma((tiles,)), dma((tiles,)), dma((tiles,)),
            dma((n_op, pieces)), dma((n_op - 1, pieces)),
        ],
        compiler_params=pltpu.CompilerParams(
            collective_id=0, has_side_effects=True, vmem_limit_bytes=60 * 1024 * 1024),
        name="sigma_step",
    )(wave, left_blocks, right_ops, delta, active.reshape(ops), sector_rows)
    return block.astype(jnp.bfloat16)


def solution(mesh):
    return jax.shard_map(
        functools.partial(on_device, mesh.shape["sector"], mesh.shape["op"]),
        mesh=mesh,
        in_specs=(
            P("sector", None),
            P("op", "sector", None),
            P("op", None, None),
            P("op"),
            P("op", "sector"),
            P("sector"),
        ),
        out_specs=P("sector", "op"),
        check_vma=False,
    )
```

```python
import functools

import jax
import jax.numpy as jnp
from jax import lax
from jax.experimental import pallas as pl
from jax.experimental.pallas import tpu as pltpu
from jax.sharding import PartitionSpec as P

MESH = pl.DeviceIdType.MESH
LANES = 128


def layout(columns, n_op):
    width = columns // n_op
    plan, most = [], 0
    for q in range(n_op):
        pieces = []
        for tile in range(columns // LANES):
            lo, hi = max(q * width, tile * LANES), min((q + 1) * width, (tile + 1) * LANES)
            if lo < hi:
                pieces.append((tile, lo - tile * LANES, hi - tile * LANES))
        placed, at = {}, 0
        for piece in sorted(pieces, key=lambda p: p[1] - p[2]):
            rows = 32 if piece[2] - piece[1] == 64 else 64
            placed[piece] = (at, rows)
            at += rows
        plan.append([p + placed[p] for p in pieces])
        most = max(most, at)
    return plan, most


def pack(block, lo, hi):
    part = block[:, lo:hi]
    if hi - lo == LANES:
        return part
    if hi - lo == 64:
        return jnp.concatenate([part[:32], part[32:]], axis=1)
    return jnp.concatenate([part, jnp.zeros((part.shape[0], LANES - hi + lo), part.dtype)], axis=1)


def unpack(rows, width):
    if width == LANES:
        return rows
    if width == 64:
        return jnp.concatenate([rows[:, :64], rows[:, 64:]], axis=0)
    return rows[:, :width]


def kernel(n_sector, n_op, wave_hbm, left_hbm, right, delta_hbm, active_hbm, live_hbm, out,
           wave, left, delta, active, live, inter, held, keep, up, down, below, above, zsend, zrecv,
           load_sem, small_sem, up_send, up_recv, down_send, down_recv, z_send, z_recv):
    s, me = lax.axis_index("sector"), lax.axis_index("op")
    ops, rows, _ = left.shape
    columns = wave.shape[1]
    tiles = columns // LANES
    chunks = tiles // 2
    plan, most = layout(columns, n_op)
    order = [tile for c in range(chunks) for tile in (c, tiles - 1 - c)]

    barrier = pltpu.get_barrier_semaphore()

    @pl.when(s > 0)
    def _():
        pl.semaphore_signal(barrier, inc=1, device_id={"sector": s - 1}, device_id_type=MESH)

    @pl.when(s < n_sector - 1)
    def _():
        pl.semaphore_signal(barrier, inc=1, device_id={"sector": s + 1}, device_id_type=MESH)

    for hop in range(1, n_op):
        pl.semaphore_signal(barrier, inc=1, device_id={"op": lax.rem(me + hop, n_op)}, device_id_type=MESH)

    small = []
    for i, (src, dst) in enumerate(((wave_hbm, wave), (left_hbm, left), (delta_hbm, delta),
                                    (active_hbm, active), (live_hbm, live))):
        small.append(pltpu.make_async_copy(src, dst, small_sem.at[i]))
        small[-1].start()

    groups = ((0, ops // 2), (ops // 2, ops))
    loads = {}
    for c in range(chunks):
        for g, (first, last) in enumerate(groups):
            for half in range(2):
                tile = order[2 * c + half]
                load = pltpu.make_async_copy(
                    right.at[first:last, :, tile * LANES:(tile + 1) * LANES],
                    held.at[c, first:last, :, half * LANES:(half + 1) * LANES],
                    load_sem.at[c, g, half])
                load.start()
                loads.setdefault((c, first), []).append(load)

    @pl.when(s == 0)
    def _():
        below[...] = jnp.zeros_like(below)

    @pl.when(s == n_sector - 1)
    def _():
        above[...] = jnp.zeros_like(above)

    for load in small:
        load.wait()
    on_rows = lax.broadcasted_iota(jnp.int32, (rows, columns), 0) < live[0]
    masked = jnp.where(on_rows, wave[...].astype(jnp.float32), 0.0).astype(jnp.bfloat16)
    stacked = left[...].reshape(ops * rows, rows)
    inter[...] = jnp.dot(stacked, masked, preferred_element_type=jnp.float32).astype(jnp.bfloat16)
    weights = [[jnp.where(delta[k] == change, active[k], 0).astype(jnp.float32) for k in range(ops)]
               for change in (0, 1, -1)]

    def to_next(i):
        return pltpu.make_async_remote_copy(
            src_ref=up.at[i], dst_ref=below.at[i], send_sem=up_send.at[i], recv_sem=up_recv.at[i],
            device_id={"sector": s + 1}, device_id_type=MESH)

    def to_previous(i):
        return pltpu.make_async_remote_copy(
            src_ref=down.at[i], dst_ref=above.at[i], send_sem=down_send.at[i], recv_sem=down_recv.at[i],
            device_id={"sector": s - 1}, device_id_type=MESH)

    def to_shard(q, index):
        _, _, _, at, size = plan[q][index]
        slot = lax.rem(me - q + n_op, n_op) - 1
        return pltpu.make_async_remote_copy(
            src_ref=zsend.at[q, at:at + size], dst_ref=zrecv.at[slot, at:at + size],
            send_sem=z_send.at[q, index], recv_sem=z_recv.at[slot, index],
            device_id={"op": q}, device_id_type=MESH)

    def from_shard(q, index, slot):
        _, _, _, at, size = plan[q][index]
        return pltpu.make_async_remote_copy(
            src_ref=zsend.at[q, at:at + size], dst_ref=zrecv.at[slot, at:at + size],
            send_sem=z_send.at[q, index], recv_sem=z_recv.at[slot, index],
            device_id={"op": lax.rem(me + slot + 1, n_op)}, device_id_type=MESH)

    def compute(c):
        sums = [None] * 3
        for k in range(ops):
            for load in loads.get((c, k), ()):
                load.wait()
            term = jnp.dot(inter[k * rows:(k + 1) * rows], held[c, k], preferred_element_type=jnp.float32)
            for d in range(3):
                scaled = term * weights[d][k]
                sums[d] = scaled if k == 0 else sums[d] + scaled
        for half in range(2):
            at = slice(half * LANES, (half + 1) * LANES)
            i = 2 * c + half
            up[i] = sums[1][:, at]
            down[i] = sums[2][:, at]
            keep[i] = sums[0][:, at]

        if c == 0:
            near = jnp.minimum(s, 1) + jnp.minimum(n_sector - 1 - s, 1)
            pl.semaphore_wait(barrier, n_op - 1 + near)

        @pl.when(s < n_sector - 1)
        def _():
            for i in (2 * c, 2 * c + 1):
                to_next(i).start()

        @pl.when(s > 0)
        def _():
            for i in (2 * c, 2 * c + 1):
                to_previous(i).start()

    def combine(i):
        @pl.when(s > 0)
        def _():
            to_next(i).wait_recv()

        @pl.when(s < n_sector - 1)
        def _():
            to_previous(i).wait_recv()

        total = keep[i] + below[i] + above[i]
        for q in range(n_op):
            for index, (tile, lo, hi, at, size) in enumerate(plan[q]):
                if tile != order[i]:
                    continue
                zsend[q, at:at + size] = pack(total, lo, hi)

                @pl.when(me != q)
                def _():
                    to_shard(q, index).start()

    for c in range(chunks):
        compute(c)
    for i in range(tiles):
        combine(i)

    for q in range(n_op):
        @pl.when(me == q)
        def _():
            for slot in range(n_op - 1):
                for index in range(len(plan[q])):
                    from_shard(q, index, slot).wait_recv()
            blocks = []
            for tile, lo, hi, at, size in plan[q]:
                whole = zsend[q, at:at + size]
                for slot in range(n_op - 1):
                    whole = whole + zrecv[slot, at:at + size]
                blocks.append(unpack(whole, hi - lo))
            block = blocks[0] if len(blocks) == 1 else jnp.concatenate(blocks, axis=1)
            shown = lax.broadcasted_iota(jnp.int32, block.shape, 0) < live[0]
            out[...] = jnp.where(shown, block, 0.0)

        @pl.when(me != q)
        def _():
            for index in range(len(plan[q])):
                to_shard(q, index).wait_send()

    @pl.when(s < n_sector - 1)
    def _():
        for i in range(tiles):
            to_next(i).wait_send()

    @pl.when(s > 0)
    def _():
        for i in range(tiles):
            to_previous(i).wait_send()


def on_device(n_sector, n_op, wave, left_blocks, right_ops, delta, active, sector_rows):
    rows, columns = wave.shape
    ops = right_ops.shape[0]
    tiles = columns // LANES
    chunks = tiles // 2
    plan, most = layout(columns, n_op)
    pieces = max(len(p) for p in plan)
    piece = pltpu.VMEM((tiles, rows, LANES), jnp.float32)
    dma = pltpu.SemaphoreType.DMA
    block = pl.pallas_call(
        functools.partial(kernel, n_sector, n_op),
        out_shape=pltpu.VMEM((rows, columns // n_op), jnp.float32),
        in_specs=[pl.BlockSpec(memory_space=pltpu.HBM)] * 6,
        out_specs=pl.BlockSpec(memory_space=pltpu.VMEM),
        scratch_shapes=[
            pltpu.VMEM(wave.shape, wave.dtype),
            pltpu.VMEM(left_blocks.shape, left_blocks.dtype),
            pltpu.SMEM((ops,), jnp.int32),
            pltpu.SMEM((ops,), jnp.int32),
            pltpu.SMEM((1,), jnp.int32),
            pltpu.VMEM((ops * rows, columns), jnp.bfloat16),
            pltpu.VMEM((chunks, ops, columns, 2 * LANES), jnp.bfloat16),
            piece, piece, piece, piece, piece,
            pltpu.VMEM((n_op, most, LANES), jnp.float32),
            pltpu.VMEM((n_op - 1, most, LANES), jnp.float32),
            dma((chunks, 2, 2)), dma((5,)),
            dma((tiles,)), dma((tiles,)), dma((tiles,)), dma((tiles,)),
            dma((n_op, pieces)), dma((n_op - 1, pieces)),
        ],
        compiler_params=pltpu.CompilerParams(
            collective_id=0, has_side_effects=True, vmem_limit_bytes=60 * 1024 * 1024),
        name="sigma_step",
    )(wave, left_blocks, right_ops, delta, active.reshape(ops), sector_rows)
    return block.astype(jnp.bfloat16)


def solution(mesh):
    return jax.shard_map(
        functools.partial(on_device, mesh.shape["sector"], mesh.shape["op"]),
        mesh=mesh,
        in_specs=(
            P("sector", None),
            P("op", "sector", None),
            P("op", None, None),
            P("op"),
            P("op", "sector"),
            P("sector"),
        ),
        out_specs=P("sector", "op"),
        check_vma=False,
    )
```

```python
import functools

import jax
import jax.numpy as jnp
from jax import lax
from jax.experimental import pallas as pl
from jax.experimental.pallas import tpu as pltpu
from jax.sharding import PartitionSpec as P

MESH = pl.DeviceIdType.MESH
LANES = 128


def layout(columns, n_op):
    width = columns // n_op
    plan, most = [], 0
    for q in range(n_op):
        pieces = []
        for tile in range(columns // LANES):
            lo, hi = max(q * width, tile * LANES), min((q + 1) * width, (tile + 1) * LANES)
            if lo < hi:
                pieces.append((tile, lo - tile * LANES, hi - tile * LANES))
        placed, at = {}, 0
        for piece in sorted(pieces, key=lambda p: p[1] - p[2]):
            rows = 32 if piece[2] - piece[1] == 64 else 64
            placed[piece] = (at, rows)
            at += rows
        plan.append([p + placed[p] for p in pieces])
        most = max(most, at)
    return plan, most


def pack(block, lo, hi):
    part = block[:, lo:hi]
    if hi - lo == LANES:
        return part
    if hi - lo == 64:
        return jnp.concatenate([part[:32], part[32:]], axis=1)
    return jnp.concatenate([part, jnp.zeros((part.shape[0], LANES - hi + lo), part.dtype)], axis=1)


def unpack(rows, width):
    if width == LANES:
        return rows
    if width == 64:
        return jnp.concatenate([rows[:, :64], rows[:, 64:]], axis=0)
    return rows[:, :width]


def kernel(n_sector, n_op, wave_hbm, left_hbm, right, delta_hbm, active_hbm, live_hbm, out,
           wave, left, delta, active, live, inter, held, keep, up, down, below, above, zsend, zrecv,
           load_sem, small_sem, up_send, up_recv, down_send, down_recv, z_send, z_recv):
    s, me = lax.axis_index("sector"), lax.axis_index("op")
    ops, rows, _ = left.shape
    columns = wave.shape[1]
    tiles = columns // LANES
    chunks = tiles // 2
    plan, most = layout(columns, n_op)
    order = [tile for c in range(chunks) for tile in (c, tiles - 1 - c)]

    barrier = pltpu.get_barrier_semaphore()

    @pl.when(s > 0)
    def _():
        pl.semaphore_signal(barrier, inc=1, device_id={"sector": s - 1}, device_id_type=MESH)

    @pl.when(s < n_sector - 1)
    def _():
        pl.semaphore_signal(barrier, inc=1, device_id={"sector": s + 1}, device_id_type=MESH)

    for hop in range(1, n_op):
        pl.semaphore_signal(barrier, inc=1, device_id={"op": lax.rem(me + hop, n_op)}, device_id_type=MESH)

    small = []
    for i, (src, dst) in enumerate(((wave_hbm, wave), (left_hbm, left), (delta_hbm, delta),
                                    (active_hbm, active), (live_hbm, live))):
        small.append(pltpu.make_async_copy(src, dst, small_sem.at[i]))
        small[-1].start()

    loads = {}
    for c in range(chunks):
        groups = ((0, ops // 2), (ops // 2, ops)) if c == 0 else ((0, ops),)
        for g, (first, last) in enumerate(groups):
            for half in range(2):
                tile = order[2 * c + half]
                load = pltpu.make_async_copy(
                    right.at[first:last, :, tile * LANES:(tile + 1) * LANES],
                    held.at[c, first:last, :, half * LANES:(half + 1) * LANES],
                    load_sem.at[c, g, half])
                load.start()
                loads.setdefault((c, first), []).append(load)

    @pl.when(s == 0)
    def _():
        below[...] = jnp.zeros_like(below)

    @pl.when(s == n_sector - 1)
    def _():
        above[...] = jnp.zeros_like(above)

    for load in small:
        load.wait()
    on_rows = lax.broadcasted_iota(jnp.int32, (rows, columns), 0) < live[0]
    masked = jnp.where(on_rows, wave[...].astype(jnp.float32), 0.0).astype(jnp.bfloat16)
    stacked = left[...].reshape(ops * rows, rows)
    inter[...] = jnp.dot(stacked, masked, preferred_element_type=jnp.float32).astype(jnp.bfloat16)
    weights = [[jnp.where(delta[k] == change, active[k], 0).astype(jnp.float32) for k in range(ops)]
               for change in (0, 1, -1)]

    def to_next(i):
        return pltpu.make_async_remote_copy(
            src_ref=up.at[i], dst_ref=below.at[i], send_sem=up_send.at[i], recv_sem=up_recv.at[i],
            device_id={"sector": s + 1}, device_id_type=MESH)

    def to_previous(i):
        return pltpu.make_async_remote_copy(
            src_ref=down.at[i], dst_ref=above.at[i], send_sem=down_send.at[i], recv_sem=down_recv.at[i],
            device_id={"sector": s - 1}, device_id_type=MESH)

    def to_shard(q, index):
        _, _, _, at, size = plan[q][index]
        slot = lax.rem(me - q + n_op, n_op) - 1
        return pltpu.make_async_remote_copy(
            src_ref=zsend.at[q, at:at + size], dst_ref=zrecv.at[slot, at:at + size],
            send_sem=z_send.at[q, index], recv_sem=z_recv.at[slot, index],
            device_id={"op": q}, device_id_type=MESH)

    def from_shard(q, index, slot):
        _, _, _, at, size = plan[q][index]
        return pltpu.make_async_remote_copy(
            src_ref=zsend.at[q, at:at + size], dst_ref=zrecv.at[slot, at:at + size],
            send_sem=z_send.at[q, index], recv_sem=z_recv.at[slot, index],
            device_id={"op": lax.rem(me + slot + 1, n_op)}, device_id_type=MESH)

    def compute(c):
        sums = [None] * 3
        for k in range(ops):
            for load in loads.get((c, k), ()):
                load.wait()
            term = jnp.dot(inter[k * rows:(k + 1) * rows], held[c, k], preferred_element_type=jnp.float32)
            for d in range(3):
                scaled = term * weights[d][k]
                sums[d] = scaled if k == 0 else sums[d] + scaled
        for half in range(2):
            at = slice(half * LANES, (half + 1) * LANES)
            i = 2 * c + half
            up[i] = sums[1][:, at]
            down[i] = sums[2][:, at]
            keep[i] = sums[0][:, at]

        if c == 0:
            near = jnp.minimum(s, 1) + jnp.minimum(n_sector - 1 - s, 1)
            pl.semaphore_wait(barrier, n_op - 1 + near)

        @pl.when(s < n_sector - 1)
        def _():
            for i in (2 * c, 2 * c + 1):
                to_next(i).start()

        @pl.when(s > 0)
        def _():
            for i in (2 * c, 2 * c + 1):
                to_previous(i).start()

    def combine(i):
        @pl.when(s > 0)
        def _():
            to_next(i).wait_recv()

        @pl.when(s < n_sector - 1)
        def _():
            to_previous(i).wait_recv()

        total = keep[i] + below[i] + above[i]
        for q in range(n_op):
            for index, (tile, lo, hi, at, size) in enumerate(plan[q]):
                if tile != order[i]:
                    continue
                zsend[q, at:at + size] = pack(total, lo, hi)

                @pl.when(me != q)
                def _():
                    to_shard(q, index).start()

    for c in range(chunks):
        compute(c)
    for i in range(tiles):
        combine(i)

    for q in range(n_op):
        @pl.when(me == q)
        def _():
            for slot in range(n_op - 1):
                for index in range(len(plan[q])):
                    from_shard(q, index, slot).wait_recv()
            blocks = []
            for tile, lo, hi, at, size in plan[q]:
                whole = zsend[q, at:at + size]
                for slot in range(n_op - 1):
                    whole = whole + zrecv[slot, at:at + size]
                blocks.append(unpack(whole, hi - lo))
            block = blocks[0] if len(blocks) == 1 else jnp.concatenate(blocks, axis=1)
            shown = lax.broadcasted_iota(jnp.int32, block.shape, 0) < live[0]
            out[...] = jnp.where(shown, block, 0.0)

        @pl.when(me != q)
        def _():
            for index in range(len(plan[q])):
                to_shard(q, index).wait_send()

    @pl.when(s < n_sector - 1)
    def _():
        for i in range(tiles):
            to_next(i).wait_send()

    @pl.when(s > 0)
    def _():
        for i in range(tiles):
            to_previous(i).wait_send()


def on_device(n_sector, n_op, wave, left_blocks, right_ops, delta, active, sector_rows):
    rows, columns = wave.shape
    ops = right_ops.shape[0]
    tiles = columns // LANES
    chunks = tiles // 2
    plan, most = layout(columns, n_op)
    pieces = max(len(p) for p in plan)
    piece = pltpu.VMEM((tiles, rows, LANES), jnp.float32)
    dma = pltpu.SemaphoreType.DMA
    block = pl.pallas_call(
        functools.partial(kernel, n_sector, n_op),
        out_shape=pltpu.VMEM((rows, columns // n_op), jnp.float32),
        in_specs=[pl.BlockSpec(memory_space=pltpu.HBM)] * 6,
        out_specs=pl.BlockSpec(memory_space=pltpu.VMEM),
        scratch_shapes=[
            pltpu.VMEM(wave.shape, wave.dtype),
            pltpu.VMEM(left_blocks.shape, left_blocks.dtype),
            pltpu.SMEM((ops,), jnp.int32),
            pltpu.SMEM((ops,), jnp.int32),
            pltpu.SMEM((1,), jnp.int32),
            pltpu.VMEM((ops * rows, columns), jnp.bfloat16),
            pltpu.VMEM((chunks, ops, columns, 2 * LANES), jnp.bfloat16),
            piece, piece, piece, piece, piece,
            pltpu.VMEM((n_op, most, LANES), jnp.float32),
            pltpu.VMEM((n_op - 1, most, LANES), jnp.float32),
            dma((chunks, 2, 2)), dma((5,)),
            dma((tiles,)), dma((tiles,)), dma((tiles,)), dma((tiles,)),
            dma((n_op, pieces)), dma((n_op - 1, pieces)),
        ],
        compiler_params=pltpu.CompilerParams(
            collective_id=0, has_side_effects=True, vmem_limit_bytes=60 * 1024 * 1024),
        name="sigma_step",
    )(wave, left_blocks, right_ops, delta, active.reshape(ops), sector_rows)
    return block.astype(jnp.bfloat16)


def solution(mesh):
    return jax.shard_map(
        functools.partial(on_device, mesh.shape["sector"], mesh.shape["op"]),
        mesh=mesh,
        in_specs=(
            P("sector", None),
            P("op", "sector", None),
            P("op", None, None),
            P("op"),
            P("op", "sector"),
            P("sector"),
        ),
        out_specs=P("sector", "op"),
        check_vma=False,
    )
```
